128 devices in a mesh: depth: 2 (over x_lo), row: 4 (over x_hi, core), col: 16 (over z, y).
Axes of the slice: x: 4 (x_hi: 2, x_lo: 2; x = x_hi * 2 + x_lo), y: 4, z: 4, core: 2. Of those that a mesh axis runs over, the one named last changes fastest.
Arguments:
- tokens: bfloat16 [4096, 4096], P(('depth', 'row'), 'col'), may hold values from -6 to 6
- gate_weight: bfloat16 [4096, 14336], P(('depth', 'row'), 'col'), may hold values from -0.09375 to 0.09375
- up_weight: bfloat16 [4096, 14336], P(('depth', 'row'), 'col'), may hold values from -0.09375 to 0.09375
- down_weight: bfloat16 [14336, 4096], P('col', ('depth', 'row')), may hold values from -0.046875 to 0.046875
- cotangent: bfloat16 [4096, 4096], P(('depth', 'row'), 'col'), may hold values from -6 to 6
Outputs:
- layer_out: bfloat16 [4096, 4096], P(('depth', 'row'), 'col')
- grad_tokens: bfloat16 [4096, 4096], P(('depth', 'row'), 'col')
- grad_gate: float32 [4096, 14336], P(('depth', 'row'), 'col')
- grad_up: float32 [4096, 14336], P(('depth', 'row'), 'col')
The draws below stay inside these ranges and needn't reach their ends.
All inputs are finite; a program needn't handle non-finite values.
Results may differ from the reference program's by a relative error of at most 0.02.
Values may be sent and summed in bfloat16 or wider, within the bound.
No kernel may reach another device: no remote copies, remote signals or barrier semaphores. Data moves between devices by JAX's collectives and lax.ppermute only.
A program may use at most 128 MiB of HBM per device.

```python
import jax
import jax.numpy as jnp
from jax import lax

D = 4096
FF = 14336
TOK_GRP = 512
TOKENS = 4096
N_DEPTH = 2
N_ROW = 4
N_COL = 16


def level_of(own_key, shape, split, least, high):
    def one(position, parts):
        heights = jax.random.uniform(jax.random.fold_in(jax.random.fold_in(own_key, 6), position), (parts,), jnp.float32, least / len(split), high / len(split))
        return jnp.repeat(jnp.exp(heights), shape[position] // parts).reshape((-1,) + (1,) * (len(shape) - position - 1))

    loudness = one(*split[0])
    for cut in split[1:]:
        loudness = loudness * one(*cut)
    return loudness


def bell_draw(key, extent, spread, bound, split=(), dtype=jnp.bfloat16):
    level = level_of(key, extent, split, -0.22, 0.18) if split else 1.0
    entries = jax.random.normal(key, extent, jnp.float32) * spread * level
    return jnp.minimum(jnp.maximum(entries, -bound), bound).astype(dtype)


def setup_inputs(seed: int = 0) -> dict:
    splits = jax.random.split(jax.random.key(seed), 6)
    return {
        "tokens": bell_draw(splits[0], (TOKENS, D), 1.0, 6.0, ((0, 8), (1, 16))),
        "gate_weight": bell_draw(splits[1], (D, FF), D ** -0.5, 0.09375, ((0, 8), (1, 16))),
        "up_weight": bell_draw(splits[2], (D, FF), D ** -0.5, 0.09375, ((0, 8), (1, 16))),
        "down_weight": bell_draw(splits[3], (FF, D), FF ** -0.5, 0.046875, ((0, 16), (1, 8))),
        "cotangent": bell_draw(splits[4], (TOKENS, D), 1.0, 6.0, ((0, 8), (1, 16))),
    }


def rounded(value):
    return lax.optimization_barrier(value.astype(jnp.bfloat16)).astype(jnp.float32)


def contract_last(left, right):
    return lax.dot_general(left, right, (((1,), (1,)), ((), ())), preferred_element_type=jnp.float32)


def contract_first(left, right):
    return lax.dot_general(left, right, (((0,), (0,)), ((), ())), preferred_element_type=jnp.float32)


def reference(tokens, gate_weight, up_weight, down_weight, cotangent):
    gate_pre = jnp.dot(tokens, gate_weight, preferred_element_type=jnp.float32)
    up_pre = jnp.dot(tokens, up_weight, preferred_element_type=jnp.float32)
    sigmoid_gate = jax.nn.sigmoid(gate_pre)
    activated = gate_pre * sigmoid_gate
    hidden = (activated * up_pre).astype(jnp.bfloat16)
    block_width = FF // N_COL
    layer_out = jnp.zeros((TOKENS, D), jnp.float32)
    for column_index in range(N_COL):
        window = slice(column_index * block_width, (column_index + 1) * block_width)
        layer_out = layer_out + rounded(jnp.dot(hidden[:, window], down_weight[window], preferred_element_type=jnp.float32))
    grad_hidden = contract_last(cotangent, down_weight)
    gate_delta = (grad_hidden * up_pre * sigmoid_gate * (1.0 + gate_pre * (1.0 - sigmoid_gate))).astype(jnp.bfloat16)
    up_delta = (grad_hidden * activated).astype(jnp.bfloat16)
    grad_tokens = jnp.zeros((TOKENS, D), jnp.float32)
    for column_index in range(N_COL):
        window = slice(column_index * block_width, (column_index + 1) * block_width)
        term = contract_last(gate_delta[:, window], gate_weight[:, window]) + contract_last(up_delta[:, window], up_weight[:, window])
        grad_tokens = grad_tokens + rounded(term)
    grad_gate = jnp.zeros((D, FF), jnp.float32)
    grad_up = jnp.zeros((D, FF), jnp.float32)
    for group_index in range(N_DEPTH * N_ROW):
        token_rows = slice(group_index * TOK_GRP, (group_index + 1) * TOK_GRP)
        grad_gate = grad_gate + rounded(contract_first(tokens[token_rows], gate_delta[token_rows]))
        grad_up = grad_up + rounded(contract_first(tokens[token_rows], up_delta[token_rows]))
    grad_scale = 1.0 / (TOKENS ** 0.5)
    return layer_out.astype(jnp.bfloat16), grad_tokens.astype(jnp.bfloat16), grad_gate * grad_scale, grad_up * grad_scale
```

```python
import jax
import jax.numpy as jnp
from jax import lax
from jax.sharding import PartitionSpec as P

GROUP = ("depth", "row")
EVERY = ("depth", "row", "col")
SIDE = 4
CORES = 2
CUTS = ((0, 512), (512, 896))


def contract_last(left, right):
    return lax.dot_general(
        left, right, (((1,), (1,)), ((), ())), preferred_element_type=jnp.float32
    )


def contract_first(left, right):
    return lax.dot_general(
        left, right, (((0,), (0,)), ((), ())), preferred_element_type=jnp.float32
    )


def group_index(x, core):
    return (x % 2) * 4 + (x // 2) * 2 + core


def ring(value):
    pairs = [
        (group_index(x, core), group_index((x + (1, -1)[core]) % SIDE, core))
        for x in range(SIDE)
        for core in range(CORES)
    ]
    return lax.ppermute(value, GROUP, pairs)


def sibling(value):
    pairs = [
        (group_index(x, core), group_index(x, 1 - core))
        for x in range(SIDE)
        for core in range(CORES)
    ]
    return lax.ppermute(value, GROUP, pairs)


def plane(value, step, first):
    pairs = []
    for x in range(SIDE):
        for core in range(CORES):
            for z in range(SIDE):
                for y in range(SIDE):
                    along_y = (core == 0) == first
                    to = (z, (y + step) % SIDE) if along_y else ((z + step) % SIDE, y)
                    base = group_index(x, core) * SIDE * SIDE
                    pairs.append((base + z * SIDE + y, base + to[0] * SIDE + to[1]))
    return lax.ppermute(value, EVERY, pairs)


def gather_axis(value, first):
    up = plane(value, 1, first)
    down = plane(value, -1, first)
    far0 = plane(up[0], 1, first)
    far1 = plane(down[1], -1, first)
    return (value[0], up[0], far0, down[0]), (value[1], up[1], far1, down[1])


def scatter_axis(parts, first):
    a, b = parts
    far0 = plane(a[2], 1, first)
    far1 = plane(b[2], -1, first)
    add = lambda *v: sum(t.astype(jnp.float32) for t in v).astype(jnp.bfloat16)
    up = plane(jnp.stack([add(a[1], far0), b[1]]), 1, first)
    down = plane(jnp.stack([a[3], add(b[3], far1)]), -1, first)
    return add(a[0], up[0], down[0]), add(b[0], up[1], down[1])


def body(tokens, gate_weight, up_weight, down_weight, cotangent):
    depth, row = lax.axis_index("depth"), lax.axis_index("row")
    core = row % 2
    x = (row // 2) * 2 + depth
    z, y = lax.axis_index("col") // SIDE, lax.axis_index("col") % SIDE
    sign = 1 - 2 * core
    own_at = [group_index((x - sign * s) % SIDE, core) for s in range(SIDE)]
    sib_at = [group_index((x + sign * s) % SIDE, 1 - core) for s in range(SIDE)]

    weights = jnp.stack([gate_weight, up_weight, down_weight.T])
    own, sib = [], []
    for lo, hi in CUTS:
        held = [weights[:, :, lo:hi]]
        for _ in range(SIDE - 1):
            held.append(ring(held[-1]))
        own.append(held)
        sib.append([sibling(piece) for piece in held])

    near = gather_axis(jnp.stack([tokens, cotangent]), True)
    whole = gather_axis(jnp.stack([jnp.stack(n) for n in near]), False)
    spread = [jnp.stack(w).reshape((SIDE * SIDE,) + tokens.shape) for w in whole]

    def place(zz, yy):
        dz, dy = (z - zz) % SIDE, (y - yy) % SIDE
        return jnp.where(core == 0, dz * SIDE + dy, dy * SIDE + dz)

    features, incoming = [
        jnp.concatenate(
            [
                lax.dynamic_index_in_dim(s, place(zz, yy), 0, keepdims=False)
                for zz in range(SIDE)
                for yy in range(SIDE)
            ],
            axis=1,
        )
        for s in spread
    ]
    rows = gate_weight.shape[0]
    cols_of = lambda v, at: lax.dynamic_slice_in_dim(v, at * rows, rows, 1)

    grad_scale = 1.0 / (tokens.shape[0] * SIDE * CORES) ** 0.5
    hidden, gate_delta, up_delta, grads = [], [], [], []
    for c in range(len(CUTS)):
        gate_pre = up_pre = grad_hidden = 0.0
        for s in range(SIDE):
            for piece, at in ((own[c][s], own_at[s]), (sib[c][s], sib_at[s])):
                f = cols_of(features, at)
                gate_pre += jnp.dot(f, piece[0], preferred_element_type=jnp.float32)
                up_pre += jnp.dot(f, piece[1], preferred_element_type=jnp.float32)
                grad_hidden += jnp.dot(
                    cols_of(incoming, at), piece[2], preferred_element_type=jnp.float32
                )
        sigmoid_gate = jax.nn.sigmoid(gate_pre)
        activated = gate_pre * sigmoid_gate
        hidden.append((activated * up_pre).astype(jnp.bfloat16))
        gate_delta.append(
            (
                grad_hidden * up_pre * sigmoid_gate * (1.0 + gate_pre * (1.0 - sigmoid_gate))
            ).astype(jnp.bfloat16)
        )
        up_delta.append((grad_hidden * activated).astype(jnp.bfloat16))
        joined = jnp.concatenate([gate_delta[c], up_delta[c]], axis=1)
        arrived = None
        for s in range(1, SIDE + 1):
            theirs = contract_first(cols_of(features, sib_at[s % SIDE]), joined)
            theirs = sibling(theirs.astype(jnp.bfloat16))
            mine = contract_first(cols_of(features, own_at[s % SIDE]), joined)
            mine = mine + theirs.astype(jnp.float32)
            if arrived is not None:
                mine = mine + arrived.astype(jnp.float32)
            if s < SIDE:
                arrived = ring(mine.astype(jnp.bfloat16))
        grads.append(mine * grad_scale)
    widths = [hi - lo for lo, hi in CUTS]
    grad_gate = jnp.concatenate([g[:, :n] for g, n in zip(grads, widths)], axis=1)
    grad_up = jnp.concatenate([g[:, n:] for g, n in zip(grads, widths)], axis=1)

    out_parts = jnp.zeros((2, SIDE * CORES, tokens.shape[0], rows), jnp.bfloat16)
    for s in range(SIDE):
        for kind, at in ((own, own_at[s]), (sib, sib_at[s])):
            layer = grad = 0.0
            for c in range(len(CUTS)):
                piece = kind[c][s]
                layer += contract_last(hidden[c], piece[2])
                grad += contract_last(gate_delta[c], piece[0])
                grad += contract_last(up_delta[c], piece[1])
            both = jnp.stack([layer, grad]).astype(jnp.bfloat16)[:, None]
            out_parts = lax.dynamic_update_slice_in_dim(out_parts, both, at, 1)
    blocks = out_parts.reshape(2, SIDE * CORES, tokens.shape[0], 2, -1)
    blocks = blocks.transpose(0, 1, 3, 2, 4).reshape((2, SIDE * SIDE) + tokens.shape)

    def block_of(part, r2, r1):
        zz = jnp.where(core == 0, z + r2, z + r1) % SIDE
        yy = jnp.where(core == 0, y + r1, y + r2) % SIDE
        return lax.dynamic_index_in_dim(blocks[part], zz * SIDE + yy, 0, keepdims=False)

    parts = [
        [jnp.stack([block_of(i, r2, r1) for r1 in range(SIDE)]) for r2 in range(SIDE)]
        for i in range(2)
    ]
    parts = scatter_axis(parts, False)
    layer_out, grad_tokens = scatter_axis(parts, True)
    return (layer_out, grad_tokens, grad_gate, grad_up)


def solution(mesh):
    in_specs = (
        P(("depth", "row"), "col"),
        P(("depth", "row"), "col"),
        P(("depth", "row"), "col"),
        P("col", ("depth", "row")),
        P(("depth", "row"), "col"),
    )
    out_specs = (
        P(("depth", "row"), "col"),
        P(("depth", "row"), "col"),
        P(("depth", "row"), "col"),
        P(("depth", "row"), "col"),
    )
    return jax.shard_map(body, mesh=mesh, in_specs=in_specs, out_specs=out_specs, check_vma=False)
```

```python
import jax
import jax.numpy as jnp
from jax import lax
from jax.experimental import pallas as pl
from jax.experimental.pallas import tpu as pltpu
from jax.sharding import PartitionSpec as P

GROUP = ("depth", "row")
EVERY = ("depth", "row", "col")
SIDE = 4
CORES = 2
CUTS = ((0, 512), (512, 896))


MIB = 1024 * 1024
LIGHT = pl.CostEstimate(flops=1, bytes_accessed=1, transcendentals=0)
HBM = pl.BlockSpec(memory_space=pltpu.HBM)
ANY = pl.BlockSpec(memory_space=pl.ANY)
VMEM = pl.BlockSpec(memory_space=pltpu.VMEM)


def after(value, *earlier):
    return lax.optimization_barrier((value, *earlier))[0]


def matmul(left, right):
    return jnp.dot(left, right, preferred_element_type=jnp.float32)


def contract_last(left, right):
    return lax.dot_general(
        left, right, (((1,), (1,)), ((), ())), preferred_element_type=jnp.float32
    )


def group_index(x, core):
    return (x % 2) * 4 + (x // 2) * 2 + core


def ring(value):
    pairs = [
        (group_index(x, core), group_index((x + (1, -1)[core]) % SIDE, core))
        for x in range(SIDE)
        for core in range(CORES)
    ]
    return lax.ppermute(value, GROUP, pairs)


def sibling(value):
    pairs = [
        (group_index(x, core), group_index(x, 1 - core))
        for x in range(SIDE)
        for core in range(CORES)
    ]
    return lax.ppermute(value, GROUP, pairs)


def plane(value, step, first):
    pairs = []
    for x in range(SIDE):
        for core in range(CORES):
            for z in range(SIDE):
                for y in range(SIDE):
                    along_y = (core == 0) == first
                    to = (z, (y + step) % SIDE) if along_y else ((z + step) % SIDE, y)
                    base = group_index(x, core) * SIDE * SIDE
                    pairs.append((base + z * SIDE + y, base + to[0] * SIDE + to[1]))
    return lax.ppermute(value, EVERY, pairs)


def seat():
    depth, row, col = (lax.axis_index(name) for name in EVERY)
    return (row // 2) * 2 + depth, row % 2, col // SIDE, col % SIDE


def held_at(step, mine):
    x, core, _, _ = seat()
    sign = 1 - 2 * core
    if mine:
        return group_index((x - sign * step + SIDE) % SIDE, core)
    return group_index((x + sign * step + SIDE) % SIDE, 1 - core)


def assemble(blocks, tokens, turn):
    arrays = []
    for array, _ in blocks.values():
        if not any(array is other for other in arrays):
            arrays.append(array)
    width = arrays[0].shape[-1]

    def kernel(*refs):
        out_ref = refs[len(arrays)]
        _, core, z, y = seat()
        for (r2, r1), (array, index) in blocks.items():
            ref = [r for r, other in zip(refs, arrays) if other is array][0]
            zz = (z + SIDE - jnp.where(core == 0, r2, r1)) % SIDE
            yy = (y + SIDE - jnp.where(core == 0, r1, r2)) % SIDE
            there = pl.ds(pl.multiple_of((zz * SIDE + yy) * width, width), width)
            out_ref[:, there] = ref[index]
            if turn:
                refs[-1][there, :] = ref[index].T

    return pl.pallas_call(
        kernel,
        out_shape=[
            jax.ShapeDtypeStruct(shape, jnp.bfloat16)
            for shape in ((tokens, SIDE * SIDE * width), (SIDE * SIDE * width, tokens))[: 1 + turn]
        ],
        in_specs=[VMEM] * len(arrays),
        out_specs=[VMEM] * (1 + turn),
        compiler_params=pltpu.CompilerParams(vmem_limit_bytes=20 * MIB),
        cost_estimate=LIGHT,
        name="assemble",
    )(*arrays)


def laid(parts):
    block, up, down, far0, far1 = parts
    blocks = {}
    for r1 in range(SIDE):
        blocks[0, r1] = (block, r1)
        blocks[1, r1] = (up, r1)
        blocks[2, r1] = (far0, r1) if r1 < 2 else (far1, r1 - 2)
        blocks[3, r1] = (down, r1)
    return blocks


def add(*values):
    return sum(v.astype(jnp.float32) for v in values).astype(jnp.bfloat16)


def forward(features, incoming, pieces, steps, wanted, carried, last):
    count = len(pieces)
    tokens = features.shape[0]
    _, rows, n = pieces[0].shape
    kinds = [m for m in range(3) if wanted[m]]
    given = [m for m in range(3) if carried[m] is not None]
    shared = wanted[0]

    def kernel(f_ref, g_ref, *refs):
        piece_refs, refs = refs[:count], refs[count:]
        carried_refs, refs = dict(zip(given, refs)), refs[len(given) :]
        outs, (f_held, g_held, w0, w1, w2, sems) = refs[:-6], refs[-6:]
        w_held = (w0, w1, w2)
        copies = [[], [], []]
        for m in kinds:
            for i, j in enumerate(wanted[m]):
                block = pl.ds(pl.multiple_of(held_at(*steps[j]) * rows, rows), rows)
                here = pl.ds(i * rows, rows)
                if m == 0:
                    copies[m].append((f_ref.at[:, block], f_held.at[:, here], sems.at[3, i]))
                if m == 2:
                    copies[m].append((g_ref.at[:, block], g_held.at[:, here], sems.at[4, i]))
                copies[m].append(
                    (piece_refs[j].at[m], w_held[m].at[here, :], sems.at[m, i])
                )
        copies = [[pltpu.make_async_copy(*c) for c in group] for group in copies]
        for group in copies:
            for c in group:
                c.start()
        results = []
        for m in kinds:
            for c in copies[m]:
                c.wait()
            result = matmul((g_held if m == 2 else f_held)[...], w_held[m][...])
            if m in given:
                result = result + carried_refs[m][...]
            if last:
                results.append(result)
            else:
                outs[len(results)][...] = result
                results.append(None)
        if last:
            gate_pre, up_pre, grad_hidden = results
            sigmoid_gate = jax.nn.sigmoid(gate_pre)
            activated = gate_pre * sigmoid_gate
            outs[0][...] = (activated * up_pre).astype(jnp.bfloat16)
            outs[1][:, :n] = (
                grad_hidden * up_pre * sigmoid_gate * (1.0 + gate_pre * (1.0 - sigmoid_gate))
            ).astype(jnp.bfloat16)
            outs[1][:, n:] = (grad_hidden * activated).astype(jnp.bfloat16)

    if last:
        out_shape = [
            jax.ShapeDtypeStruct((tokens, n), jnp.bfloat16),
            jax.ShapeDtypeStruct((tokens, 2 * n), jnp.bfloat16),
        ]
    else:
        out_shape = [jax.ShapeDtypeStruct((tokens, n), jnp.float32)] * len(kinds)
    depths = [max(len(w), 1) * rows for w in wanted]
    return pl.pallas_call(
        kernel,
        out_shape=out_shape,
        in_specs=[ANY] * 2 + [HBM] * count + [VMEM] * len(given),
        out_specs=[VMEM] * len(out_shape),
        scratch_shapes=[
            pltpu.VMEM((tokens, depths[0]), jnp.bfloat16),
            pltpu.VMEM((tokens, depths[2]), jnp.bfloat16),
        ]
        + [pltpu.VMEM((depth, n), jnp.bfloat16) for depth in depths]
        + [pltpu.SemaphoreType.DMA((5, count))],
        compiler_params=pltpu.CompilerParams(vmem_limit_bytes=26 * MIB),
        cost_estimate=LIGHT,
        name="forward_last" if last else "forward_part",
    )(features, incoming, *pieces, *(carried[m] for m in given))


def outer(turned, joined, steps):
    tokens, width = joined.shape
    count = len(steps)
    rows = turned.shape[0] // (SIDE * CORES)

    def kernel(t_ref, j_ref, theirs_ref, mine_ref, held, sems):
        now = pl.program_id(0)

        @pl.when(now == 0)
        def _():
            for i in range(count):
                for mine in (0, 1):
                    block = pl.ds(pl.multiple_of(held_at(steps[i], mine) * rows, rows), rows)
                    pltpu.make_async_copy(
                        t_ref.at[block, :], held.at[2 * i + mine], sems.at[2 * i + mine]
                    ).start()

        for mine, ref in enumerate((theirs_ref, mine_ref)):
            slot = 2 * now + mine
            pltpu.make_async_copy(
                t_ref.at[pl.ds(0, rows), :], held.at[slot], sems.at[slot]
            ).wait()
            ref[0] = matmul(held[slot], j_ref[...]).astype(jnp.bfloat16)

    spec = pl.BlockSpec((1, rows, width), lambda i: (i, 0, 0))
    return pl.pallas_call(
        kernel,
        grid=(count,),
        out_shape=[jax.ShapeDtypeStruct((count, rows, width), jnp.bfloat16)] * 2,
        in_specs=[ANY, pl.BlockSpec((tokens, width), lambda i: (0, 0))],
        out_specs=[spec, spec],
        scratch_shapes=[
            pltpu.VMEM((2 * count, rows, tokens), jnp.bfloat16),
            pltpu.SemaphoreType.DMA((2 * count,)),
        ],
        compiler_params=pltpu.CompilerParams(vmem_limit_bytes=16 * MIB),
        cost_estimate=LIGHT,
        name="outer_product",
    )(turned, joined)


def partial_blocks(aheads, hidden, joined, pieces, base):
    tokens, n = hidden.shape
    count = len(pieces)
    total = SIDE * len(aheads)
    width = pieces[0].shape[1] // 2
    arrays = base[:2]

    def kernel(hid_ref, join_ref, *refs):
        base_refs, refs = refs[: len(arrays)], refs[len(arrays) :]
        piece_refs, refs = refs[:count], refs[count:]
        layer_ref, grad_ref, held, sems = refs
        now = pl.program_id(0)

        @pl.when(now == 0)
        def _():
            x, core, z, y = seat()
            sign = 1 - 2 * core
            for r in range(total):
                ahead = aheads[r // SIDE]
                zz = jnp.where(core == 0, z + ahead, z + r % SIDE) % SIDE
                yy = jnp.where(core == 0, y + r % SIDE, y + ahead) % SIDE
                block = (zz * SIDE + yy) // 2
                x_of = ((block % 4) // 2) * 2 + block // 4
                core_of = block % 2
                step = (sign * (x - x_of) + SIDE) % SIDE
                piece = jnp.where(core_of == core, step, SIDE + (SIDE - step) % SIDE)
                part = pl.ds(pl.multiple_of((yy % 2) * width, width), width)
                for i in range(count):

                    @pl.when(piece == i)
                    def _():
                        pltpu.make_async_copy(
                            piece_refs[i].at[:, part, :], held.at[r], sems.at[r]
                        ).start()

        pltpu.make_async_copy(
            piece_refs[0].at[:, pl.ds(0, width), :], held.at[now], sems.at[now]
        ).wait()
        layer = contract_last(hid_ref[...], held[now, 2])
        grad = contract_last(join_ref[:, :n], held[now, 0])
        grad = grad + contract_last(join_ref[:, n:], held[now, 1])
        if arrays:
            layer = layer + base_refs[0][0].astype(jnp.float32)
            grad = grad + base_refs[1][0].astype(jnp.float32)
        layer_ref[0] = layer.astype(jnp.bfloat16)
        grad_ref[0] = grad.astype(jnp.bfloat16)

    spec = pl.BlockSpec((1, tokens, width), lambda i: (i, 0, 0))
    start = base[2] if base else 0
    base_spec = pl.BlockSpec((1, tokens, width), lambda i: (i + start, 0, 0))
    return pl.pallas_call(
        kernel,
        grid=(total,),
        out_shape=[jax.ShapeDtypeStruct((total, tokens, width), jnp.bfloat16)] * 2,
        in_specs=[pl.BlockSpec((tokens, k * n), lambda i: (0, 0)) for k in (1, 2)]
        + [base_spec] * len(arrays)
        + [HBM] * count,
        out_specs=[spec, spec],
        scratch_shapes=[
            pltpu.VMEM((total, 3, width, n), jnp.bfloat16),
            pltpu.SemaphoreType.DMA((total,)),
        ],
        compiler_params=pltpu.CompilerParams(vmem_limit_bytes=22 * MIB),
        cost_estimate=LIGHT,
        name="partial_blocks",
    )(hidden, joined, *arrays, *pieces)


def body(tokens, gate_weight, up_weight, down_weight, cotangent):
    count = tokens.shape[0]
    weights = jnp.stack([gate_weight, up_weight, down_weight.T])
    own = [[weights[:, :, lo:hi]] for lo, hi in CUTS]
    sib = [[], []]
    early = [(s, m) for s in range(SIDE - 1) for m in (True, False)]
    late = [(SIDE - 1, m) for m in (True, False)]
    take = lambda c, steps: [(own if m else sib)[c][s] for s, m in steps]

    both = jnp.stack([tokens, cotangent])
    near = [both] + [plane(both, step, True) for step in (1, 2, -1)]
    own[0].append(ring(own[0][0]))

    over = (own[0][1], *near[1:])
    tok = [jnp.stack([v[0] for v in near])]
    own[0].append(ring(after(own[0][1], *over)))
    sib[0] += [sibling(after(own[0][s], *over)) for s in (0, 1)]
    tok += [plane(after(tok[0], *over), step, False) for step in (1, -1)]

    over = (own[0][2], *sib[0], *tok[1:])
    own[0].append(ring(after(own[0][2], *over)))
    tok.append(plane(after(tok[1][:2], *over), 1, False))
    tok.append(plane(after(tok[2][2:], *over), -1, False))
    cot = [jnp.stack([v[1] for v in near])]
    own[1].append(ring(after(own[1][0], *over)))
    sib[0].append(sibling(after(own[0][2], *tok[3:])))
    cot += [plane(after(cot[0], *tok[3:]), step, False) for step in (1, -1)]
    features, turned = assemble(laid(tok), count, True)
    steps = early + late
    most, rest, none = tuple(range(6)), (6, 7), (None,) * 3
    sums0 = forward(
        features, cot[0], take(0, early), early, (most, most, ()), none, False
    )
    cot.append(plane(after(cot[1][:2], features), 1, False))
    cot.append(plane(after(cot[2][2:], features), -1, False))

    over = (own[0][3], own[1][1], sib[0][2], *cot[3:], sums0[0])
    own[1].append(ring(after(own[1][1], *over)))
    sib[0].append(sibling(after(own[0][3], *over)))
    sib[1] += [sibling(after(own[1][s], *over)) for s in (0, 1)]
    (incoming,) = assemble(laid(cot), count, False)
    hid0, join0 = forward(
        features,
        after(incoming, sib[0][3]),
        take(0, steps),
        steps,
        (rest, rest, most + rest),
        (*sums0, None),
        True,
    )
    theirs0, mine0 = outer(turned, join0, (1, 2, 3, 0))

    over = (own[1][2], theirs0, *sib[1])
    own[1].append(ring(after(own[1][2], *over)))
    got0 = sibling(after(theirs0, *over))
    sib[1].append(sibling(after(own[1][2], *over)))
    pieces0 = own[0] + sib[0]
    base = partial_blocks((2, 1, 3, 0), after(hid0, *over), join0, pieces0, ())

    over = (own[1][3], got0, *sib[1], base[0])
    sib[1].append(sibling(after(own[1][3], *over)))
    sent0 = add(after(mine0[0], *over), got0[0])
    came0 = ring(sent0)
    sums1 = forward(
        after(features, sib[1][2], sent0), incoming, take(1, early), early, (most,) * 3, none, False
    )
    sums1 = (after(sums1[0], sib[1][3]), *sums1[1:])
    hid1, join1 = forward(features, incoming, take(1, late), late, ((0, 1),) * 3, sums1, True)
    theirs1, mine1 = outer(turned, join1, (1,))
    got1 = sibling(theirs1)
    pieces1 = own[1] + sib[1]
    layer, grad = [None] * SIDE, [None] * SIDE

    def second_part(ahead, *earlier):
        where = SIDE * (2, 1, 3, 0).index(ahead)
        layer[ahead], grad[ahead] = partial_blocks(
            (ahead,), after(hid1, *earlier), join1, pieces1, (*base, where)
        )

    second_part(2, mine1)

    over = (came0, got1, layer[2])
    far_layer, far_grad = plane(after(layer[2], *over), 1, False), plane(grad[2], -1, False)
    sent0 = add(mine0[1], got0[1], after(came0, *over))
    sent1 = add(mine1[0], after(got1, *over)[0])
    came0, came1 = ring(sent0), ring(sent1)
    second_part(1, sent0, sent1)
    up_grad = plane(grad[1], 1, False)
    second_part(3, layer[1])
    down_layer = plane(layer[3], -1, False)
    rest1, own_rest1 = outer(turned, after(join1, layer[3]), (2, 3, 0))

    over = (came0, came1, far_layer, far_grad, own_rest1)
    got_rest1 = sibling(after(rest1, *over))
    up_layer = plane(add(layer[1], after(far_layer, *over)), 1, False)
    down_grad = plane(add(grad[3], after(far_grad, *over)), -1, False)
    sent0 = add(mine0[2], got0[2], after(came0, *over))
    came0 = ring(sent0)
    sent1 = add(own_rest1[0], got_rest1[0], came1)
    came1 = ring(sent1)
    second_part(0, sent1)

    over = (came1, layer[0], up_grad, down_layer, up_layer, down_grad)
    sent1 = add(own_rest1[1], got_rest1[1], after(came1, *over))
    came1 = ring(sent1)
    layer = add(layer[0], after(up_layer, sent1), down_layer)
    grad = add(grad[0], up_grad, after(down_grad, sent1))
    total = jnp.stack([layer, grad], axis=1)
    came_near = [plane(total[r1], step, True) for r1, step in ((1, 1), (2, 2), (3, -1))]

    scale = 1.0 / (count * SIDE * CORES) ** 0.5
    grads = [
        sum(v.astype(jnp.float32) for v in terms) * scale
        for terms in ((mine0[3], got0[3], came0), (own_rest1[2], got_rest1[2], came1))
    ]
    layer_out, grad_tokens = [add(total[0, i], *(v[i] for v in came_near)) for i in range(2)]
    widths = [hi - lo for lo, hi in CUTS]
    grad_gate = jnp.concatenate([g[:, :n] for g, n in zip(grads, widths)], axis=1)
    grad_up = jnp.concatenate([g[:, n:] for g, n in zip(grads, widths)], axis=1)
    return (layer_out, grad_tokens, grad_gate, grad_up)


def solution(mesh):
    in_specs = (
        P(("depth", "row"), "col"),
        P(("depth", "row"), "col"),
        P(("depth", "row"), "col"),
        P("col", ("depth", "row")),
        P(("depth", "row"), "col"),
    )
    out_specs = (
        P(("depth", "row"), "col"),
        P(("depth", "row"), "col"),
        P(("depth", "row"), "col"),
        P(("depth", "row"), "col"),
    )
    return jax.shard_map(body, mesh=mesh, in_specs=in_specs, out_specs=out_specs, check_vma=False)
```

```python
import jax
import jax.numpy as jnp
from jax import lax
from jax.experimental import pallas as pl
from jax.experimental.pallas import tpu as pltpu
from jax.sharding import PartitionSpec as P

GROUP = ("depth", "row")
EVERY = ("depth", "row", "col")
SIDE = 4
CORES = 2
CUTS = ((0, 512), (512, 896))


MIB = 1024 * 1024
LIGHT = pl.CostEstimate(flops=1, bytes_accessed=1, transcendentals=0)
HBM = pl.BlockSpec(memory_space=pltpu.HBM)
ANY = pl.BlockSpec(memory_space=pl.ANY)
VMEM = pl.BlockSpec(memory_space=pltpu.VMEM)


def after(value, *earlier):
    return lax.optimization_barrier((value, *earlier))[0]


def matmul(left, right):
    return jnp.dot(left, right, preferred_element_type=jnp.float32)


def contract_last(left, right):
    return lax.dot_general(
        left, right, (((1,), (1,)), ((), ())), preferred_element_type=jnp.float32
    )


def group_index(x, core):
    return (x % 2) * 4 + (x // 2) * 2 + core


def ring(value):
    pairs = [
        (group_index(x, core), group_index((x + (1, -1)[core]) % SIDE, core))
        for x in range(SIDE)
        for core in range(CORES)
    ]
    return lax.ppermute(value, GROUP, pairs)


def sibling(value):
    pairs = [
        (group_index(x, core), group_index(x, 1 - core))
        for x in range(SIDE)
        for core in range(CORES)
    ]
    return lax.ppermute(value, GROUP, pairs)


def plane(value, step, first):
    pairs = []
    for x in range(SIDE):
        for core in range(CORES):
            for z in range(SIDE):
                for y in range(SIDE):
                    along_y = (core == 0) == first
                    to = (z, (y + step) % SIDE) if along_y else ((z + step) % SIDE, y)
                    base = group_index(x, core) * SIDE * SIDE
                    pairs.append((base + z * SIDE + y, base + to[0] * SIDE + to[1]))
    return lax.ppermute(value, EVERY, pairs)


def seat():
    depth, row, col = (lax.axis_index(name) for name in EVERY)
    return (row // 2) * 2 + depth, row % 2, col // SIDE, col % SIDE


def held_at(step, mine):
    x, core, _, _ = seat()
    sign = 1 - 2 * core
    if mine:
        return group_index((x - sign * step + SIDE) % SIDE, core)
    return group_index((x + sign * step + SIDE) % SIDE, 1 - core)


def assemble(blocks, tokens, turn):
    arrays = []
    for array, _ in blocks.values():
        if not any(array is other for other in arrays):
            arrays.append(array)
    width = arrays[0].shape[-1]

    def kernel(*refs):
        out_ref = refs[len(arrays)]
        _, core, z, y = seat()
        for (r2, r1), (array, index) in blocks.items():
            ref = [r for r, other in zip(refs, arrays) if other is array][0]
            zz = (z + SIDE - jnp.where(core == 0, r2, r1)) % SIDE
            yy = (y + SIDE - jnp.where(core == 0, r1, r2)) % SIDE
            there = pl.ds(pl.multiple_of((zz * SIDE + yy) * width, width), width)
            lanes = pl.ds(pl.multiple_of((yy % 2) * width, width), width)
            out_ref[(zz * SIDE + yy) // 2, :, lanes] = ref[index]
            if turn:
                refs[-1][there, :] = ref[index].T

    return pl.pallas_call(
        kernel,
        out_shape=[
            jax.ShapeDtypeStruct(shape, jnp.bfloat16)
            for shape in ((8, tokens, 2 * width), (SIDE * SIDE * width, tokens))[: 1 + turn]
        ],
        in_specs=[VMEM] * len(arrays),
        out_specs=[VMEM] * (1 + turn),
        compiler_params=pltpu.CompilerParams(vmem_limit_bytes=20 * MIB),
        cost_estimate=LIGHT,
        name="assemble",
    )(*arrays)


def laid(parts):
    block, up, down, far0, far1 = parts
    blocks = {}
    for r1 in range(SIDE):
        blocks[0, r1] = (block, r1)
        blocks[1, r1] = (up, r1)
        blocks[2, r1] = (far0, r1) if r1 < 2 else (far1, r1 - 2)
        blocks[3, r1] = (down, r1)
    return blocks


def add(*values):
    return sum(v.astype(jnp.float32) for v in values).astype(jnp.bfloat16)


def forward(features, incoming, pieces, steps, wanted, carried, last):
    count = len(pieces)
    tokens = features.shape[1]
    _, rows, n = pieces[0].shape
    kinds = [m for m in range(3) if wanted[m]]
    given = [m for m in range(3) if carried[m] is not None]
    shared = wanted[0]

    def kernel(f_ref, g_ref, *refs):
        piece_refs, refs = refs[:count], refs[count:]
        carried_refs, refs = dict(zip(given, refs)), refs[len(given) :]
        outs, (f_held, g_held, w0, w1, w2, sems) = refs[:-6], refs[-6:]
        w_held = (w0, w1, w2)
        copies = [[], [], []]
        for m in kinds:
            for i, j in enumerate(wanted[m]):
                block = held_at(*steps[j])
                here = pl.ds(i * rows, rows)
                if m == 0:
                    copies[m].append((f_ref.at[block], f_held.at[:, here], sems.at[3, i]))
                if m == 2:
                    copies[m].append((g_ref.at[block], g_held.at[:, here], sems.at[4, i]))
                copies[m].append(
                    (piece_refs[j].at[m], w_held[m].at[here, :], sems.at[m, i])
                )
        copies = [[pltpu.make_async_copy(*c) for c in group] for group in copies]
        for group in copies:
            for c in group:
                c.start()
        results = []
        for m in kinds:
            for c in copies[m]:
                c.wait()
            result = matmul((g_held if m == 2 else f_held)[...], w_held[m][...])
            if m in given:
                result = result + carried_refs[m][...]
            if last:
                results.append(result)
            else:
                outs[len(results)][...] = result
                results.append(None)
        if last:
            gate_pre, up_pre, grad_hidden = results
            sigmoid_gate = jax.nn.sigmoid(gate_pre)
            activated = gate_pre * sigmoid_gate
            outs[0][...] = (activated * up_pre).astype(jnp.bfloat16)
            outs[1][:, :n] = (
                grad_hidden * up_pre * sigmoid_gate * (1.0 + gate_pre * (1.0 - sigmoid_gate))
            ).astype(jnp.bfloat16)
            outs[1][:, n:] = (grad_hidden * activated).astype(jnp.bfloat16)

    if last:
        out_shape = [
            jax.ShapeDtypeStruct((tokens, n), jnp.bfloat16),
            jax.ShapeDtypeStruct((tokens, 2 * n), jnp.bfloat16),
        ]
    else:
        out_shape = [jax.ShapeDtypeStruct((tokens, n), jnp.float32)] * len(kinds)
    depths = [max(len(w), 1) * rows for w in wanted]
    return pl.pallas_call(
        kernel,
        out_shape=out_shape,
        in_specs=[ANY] * 2 + [HBM] * count + [VMEM] * len(given),
        out_specs=[VMEM] * len(out_shape),
        scratch_shapes=[
            pltpu.VMEM((tokens, depths[0]), jnp.bfloat16),
            pltpu.VMEM((tokens, depths[2]), jnp.bfloat16),
        ]
        + [pltpu.VMEM((depth, n), jnp.bfloat16) for depth in depths]
        + [pltpu.SemaphoreType.DMA((5, count))],
        compiler_params=pltpu.CompilerParams(vmem_limit_bytes=26 * MIB),
        cost_estimate=LIGHT,
        name="forward_last" if last else "forward_part",
    )(features, incoming, *pieces, *(carried[m] for m in given))


def outer(turned, joined, steps):
    tokens, width = joined.shape
    count = len(steps)
    rows = turned.shape[0] // (SIDE * CORES)

    def kernel(t_ref, j_ref, first_ref, rest_ref, mine_ref, held, sems):
        now = pl.program_id(0)

        @pl.when(now == 0)
        def _():
            for i in range(count):
                for mine in (0, 1):
                    block = pl.ds(pl.multiple_of(held_at(steps[i], mine) * rows, rows), rows)
                    pltpu.make_async_copy(
                        t_ref.at[block, :], held.at[2 * i + mine], sems.at[2 * i + mine]
                    ).start()

        for mine in (0, 1):
            slot = 2 * now + mine
            pltpu.make_async_copy(
                t_ref.at[pl.ds(0, rows), :], held.at[slot], sems.at[slot]
            ).wait()
            result = matmul(held[slot], j_ref[...]).astype(jnp.bfloat16)
            if mine:
                mine_ref[0] = result
            else:

                @pl.when(now == 0)
                def _():
                    first_ref[...] = result

                @pl.when(now > 0)
                def _():
                    rest_ref[0] = result

    shape = lambda *dims: jax.ShapeDtypeStruct((*dims, rows, width), jnp.bfloat16)
    return pl.pallas_call(
        kernel,
        grid=(count,),
        out_shape=[shape(), shape(count - 1), shape(count)],
        in_specs=[ANY, pl.BlockSpec((tokens, width), lambda i: (0, 0))],
        out_specs=[
            pl.BlockSpec((rows, width), lambda i: (0, 0)),
            pl.BlockSpec((1, rows, width), lambda i: (jnp.maximum(i - 1, 0), 0, 0)),
            pl.BlockSpec((1, rows, width), lambda i: (i, 0, 0)),
        ],
        scratch_shapes=[
            pltpu.VMEM((2 * count, rows, tokens), jnp.bfloat16),
            pltpu.SemaphoreType.DMA((2 * count,)),
        ],
        compiler_params=pltpu.CompilerParams(vmem_limit_bytes=20 * MIB),
        cost_estimate=LIGHT,
        name="outer_product",
    )(turned, joined)


def partial_blocks(ahead, firsts, chunks, extra=None, extra_at=0):
    tokens = chunks[0][0].shape[0]
    widths = [hidden.shape[1] for hidden, _, _ in chunks]
    count = len(chunks[0][2])
    total = len(firsts)
    width = chunks[0][2][0].shape[1] // 2
    given = [] if extra is None else [extra]

    def kernel(*refs):
        act_refs, refs = refs[: 2 * len(chunks)], refs[2 * len(chunks) :]
        extra_refs, refs = refs[: len(given)], refs[len(given) :]
        piece_refs, refs = refs[: count * len(chunks)], refs[count * len(chunks) :]
        out_ref, *held, sems = refs
        now = pl.program_id(0)

        @pl.when(now == 0)
        def _():
            x, core, z, y = seat()
            sign = 1 - 2 * core
            for i, r in enumerate(firsts):
                zz = jnp.where(core == 0, z + ahead, z + r) % SIDE
                yy = jnp.where(core == 0, y + r, y + ahead) % SIDE
                block = (zz * SIDE + yy) // 2
                x_of = ((block % 4) // 2) * 2 + block // 4
                core_of = block % 2
                step = (sign * (x - x_of) + SIDE) % SIDE
                piece = jnp.where(core_of == core, step, SIDE + (SIDE - step) % SIDE)
                part = pl.ds(pl.multiple_of((yy % 2) * width, width), width)
                for p in range(count):

                    @pl.when(piece == p)
                    def _():
                        for c in range(len(chunks)):
                            pltpu.make_async_copy(
                                piece_refs[c * count + p].at[:, part, :],
                                held[c].at[i],
                                sems.at[c, i],
                            ).start()

        layer = grad = None
        for c, n in enumerate(widths):
            hid_ref, join_ref = act_refs[2 * c : 2 * c + 2]
            pltpu.make_async_copy(
                piece_refs[c * count].at[:, pl.ds(0, width), :], held[c].at[now], sems.at[c, now]
            ).wait()
            one = contract_last(hid_ref[...], held[c][now, 2])
            two = contract_last(join_ref[:, :n], held[c][now, 0])
            two = two + contract_last(join_ref[:, n:], held[c][now, 1])
            layer = one if layer is None else layer + one
            grad = two if grad is None else grad + two
        if given:
            counts = (now >= extra_at) & (now < extra_at + extra.shape[0])
            counts = jnp.where(counts, 1.0, 0.0)
            layer = layer + counts * extra_refs[0][0, 0].astype(jnp.float32)
            grad = grad + counts * extra_refs[0][0, 1].astype(jnp.float32)
        out_ref[0, 0] = layer.astype(jnp.bfloat16)
        out_ref[0, 1] = grad.astype(jnp.bfloat16)

    def extra_block(i):
        return jnp.clip(i - extra_at, 0, extra.shape[0] - 1), 0, 0, 0

    block = (1, 2, tokens, width)
    acts = [(act, pl.BlockSpec(act.shape, lambda i: (0, 0))) for c in chunks for act in c[:2]]
    return pl.pallas_call(
        kernel,
        grid=(total,),
        out_shape=jax.ShapeDtypeStruct((total, 2, tokens, width), jnp.bfloat16),
        in_specs=[s for _, s in acts]
        + [pl.BlockSpec(block, extra_block)] * len(given)
        + [HBM] * (count * len(chunks)),
        out_specs=pl.BlockSpec(block, lambda i: (i, 0, 0, 0)),
        scratch_shapes=[pltpu.VMEM((total, 3, width, n), jnp.bfloat16) for n in widths]
        + [pltpu.SemaphoreType.DMA((len(chunks), total))],
        compiler_params=pltpu.CompilerParams(vmem_limit_bytes=20 * MIB),
        cost_estimate=LIGHT,
        name="partial_blocks",
    )(*[act for act, _ in acts], *given, *[p for c in chunks for p in c[2]])


def body(tokens, gate_weight, up_weight, down_weight, cotangent):
    count = tokens.shape[0]
    weights = jnp.stack([gate_weight, up_weight, down_weight.T])
    own = [[weights[:, :, lo:hi]] for lo, hi in CUTS]
    sib = [[], []]
    early = [(s, m) for s in range(SIDE - 1) for m in (True, False)]
    late = [(SIDE - 1, m) for m in (True, False)]
    take = lambda c, steps: [(own if m else sib)[c][s] for s, m in steps]

    both = jnp.stack([tokens, cotangent])
    near = [both] + [plane(both, step, True) for step in (1, 2, -1)]
    own[0].append(ring(own[0][0]))

    over = (own[0][1], *near[1:])
    tok = [jnp.stack([v[0] for v in near])]
    own[0].append(ring(after(own[0][1], *over)))
    sib[0] += [sibling(after(own[0][s], *over)) for s in (0, 1)]
    tok += [plane(after(tok[0], *over), step, False) for step in (1, -1)]

    over = (own[0][2], *sib[0], *tok[1:])
    own[0].append(ring(after(own[0][2], *over)))
    tok.append(plane(after(tok[1][:2], *over), 1, False))
    tok.append(plane(after(tok[2][2:], *over), -1, False))
    sib[0].append(sibling(after(own[0][2], *tok[3:])))
    own[1].append(ring(after(own[1][0], own[0][3])))
    cot = [jnp.stack([v[1] for v in near])]
    cot += [plane(after(cot[0], *tok[3:]), step, False) for step in (1, -1)]
    features, turned = assemble(laid(tok), count, True)
    steps = early + late
    most, rest, none = tuple(range(6)), (6, 7), (None,) * 3
    sums0 = forward(
        features, cot[0], take(0, early), early, (most, most, ()), none, False
    )
    cot.append(plane(after(cot[1][:2], features), 1, False))
    cot.append(plane(after(cot[2][2:], features), -1, False))

    over = (own[0][3], own[1][1], sib[0][2], *cot[3:], sums0[0])
    own[1].append(ring(after(own[1][1], *over)))
    sib[0].append(sibling(after(own[0][3], *over)))
    sib[1] += [sibling(after(own[1][s], *over)) for s in (0, 1)]
    (incoming,) = assemble(laid(cot), count, False)
    hid0, join0 = forward(
        features,
        after(incoming, sib[0][3]),
        take(0, steps),
        steps,
        (rest, rest, most + rest),
        (*sums0, None),
        True,
    )
    first0, rest0, mine0 = outer(turned, join0, (1, 2, 3, 0))

    over = (own[1][2], mine0, *sib[1])
    own[1].append(ring(after(own[1][2], *over)))
    got0 = sibling(after(first0, *over))
    sib[1].append(sibling(after(own[1][2], *over)))
    sent0 = add(mine0[0], got0)
    chunk0 = (hid0, join0, own[0] + sib[0])
    sums1 = forward(
        after(features, sent0, sib[1][2]),
        incoming,
        take(1, early),
        early,
        (most,) * 3,
        none,
        False,
    )

    over = (own[1][3], sent0, *sib[1], sums1[0])
    sib[1].append(sibling(after(own[1][3], *over)))
    came0 = ring(after(sent0, *over))
    got0 = sibling(after(rest0, *over))
    sums1 = (after(sums1[0], sib[1][3]), *sums1[1:])
    hid1, join1 = forward(features, incoming, take(1, late), late, ((0, 1),) * 3, sums1, True)
    chunk1 = (hid1, join1, own[1] + sib[1])

    def blocks(ahead, firsts, earlier, *extra):
        chunks = [(after(hid0, *earlier), *chunk0[1:]), chunk1]
        return partial_blocks(ahead, firsts, chunks, *extra)

    low = blocks(2, (0, 1), ())
    high = blocks(2, (2, 3), (low,))

    over = (came0, got0, high)
    far_up = plane(after(low, *over), 1, False)
    far_down = plane(after(high, *over), -1, False)
    sent0 = add(mine0[1], got0[0], after(came0, *over))
    came0 = ring(sent0)
    first1, rest1, mine1 = outer(turned, after(join1, sent0), (1, 2, 3, 0))
    got1 = sibling(first1)
    whole = tuple(range(SIDE))
    here = blocks(0, whole, (mine1,))

    over = (came0, got1, far_up, far_down, here)
    sent0 = add(mine0[2], got0[1], after(came0, *over))
    sent1 = add(mine1[0], after(got1, *over))
    came0, came1 = ring(sent0), ring(sent1)
    got1 = sibling(after(rest1, *over))
    behind = blocks(1, whole, (sent0, sent1), far_up, 0)
    up = plane(behind, 1, False)
    front = blocks(3, whole, (behind, got1), far_down, 2)
    down = plane(front, -1, False)

    over = (came0, came1, front)
    sent1 = add(mine1[1], got1[0], after(came1, *over))
    came1 = ring(sent1)
    total = add(here, after(up, sent1), down)
    came_near = [plane(total[r1], step, True) for r1, step in ((1, 1), (2, 2), (3, -1))]
    sent1 = add(mine1[2], got1[1], came1)
    came1 = ring(sent1)

    scale = 1.0 / (count * SIDE * CORES) ** 0.5
    grads = [
        sum(v.astype(jnp.float32) for v in terms) * scale
        for terms in ((mine0[3], got0[2], came0), (mine1[3], got1[2], came1))
    ]
    widths = [hi - lo for lo, hi in CUTS]
    grad_gate = jnp.concatenate([g[:, :n] for g, n in zip(grads, widths)], axis=1)
    grad_up = jnp.concatenate([g[:, n:] for g, n in zip(grads, widths)], axis=1)
    total = after(total[0], grad_gate, grad_up)
    layer_out, grad_tokens = [add(total[i], *(v[i] for v in came_near)) for i in range(2)]
    return (layer_out, grad_tokens, grad_gate, grad_up)


def solution(mesh):
    in_specs = (
        P(("depth", "row"), "col"),
        P(("depth", "row"), "col"),
        P(("depth", "row"), "col"),
        P("col", ("depth", "row")),
        P(("depth", "row"), "col"),
    )
    out_specs = (
        P(("depth", "row"), "col"),
        P(("depth", "row"), "col"),
        P(("depth", "row"), "col"),
        P(("depth", "row"), "col"),
    )
    return jax.shard_map(body, mesh=mesh, in_specs=in_specs, out_specs=out_specs, check_vma=False)
```

```python
import jax
import jax.numpy as jnp
from jax import lax
from jax.experimental import pallas as pl
from jax.experimental.pallas import tpu as pltpu
from jax.sharding import PartitionSpec as P

GROUP = ("depth", "row")
EVERY = ("depth", "row", "col")
SIDE = 4
CORES = 2
CUTS = ((0, 512), (512, 896))


MIB = 1024 * 1024
LIGHT = pl.CostEstimate(flops=1, bytes_accessed=1, transcendentals=0)
HBM = pl.BlockSpec(memory_space=pltpu.HBM)
ANY = pl.BlockSpec(memory_space=pl.ANY)
VMEM = pl.BlockSpec(memory_space=pltpu.VMEM)


def after(value, *earlier):
    return lax.optimization_barrier((value, *earlier))[0]


def matmul(left, right):
    return jnp.dot(left, right, preferred_element_type=jnp.float32)


def contract_last(left, right):
    return lax.dot_general(
        left, right, (((1,), (1,)), ((), ())), preferred_element_type=jnp.float32
    )


def group_index(x, core):
    return (x % 2) * 4 + (x // 2) * 2 + core


def ring(value):
    pairs = [
        (group_index(x, core), group_index((x + (1, -1)[core]) % SIDE, core))
        for x in range(SIDE)
        for core in range(CORES)
    ]
    return lax.ppermute(value, GROUP, pairs)


def sibling(value):
    pairs = [
        (group_index(x, core), group_index(x, 1 - core))
        for x in range(SIDE)
        for core in range(CORES)
    ]
    return lax.ppermute(value, GROUP, pairs)


def plane(value, step, first):
    pairs = []
    for x in range(SIDE):
        for core in range(CORES):
            for z in range(SIDE):
                for y in range(SIDE):
                    along_y = (core == 0) == first
                    to = (z, (y + step) % SIDE) if along_y else ((z + step) % SIDE, y)
                    base = group_index(x, core) * SIDE * SIDE
                    pairs.append((base + z * SIDE + y, base + to[0] * SIDE + to[1]))
    return lax.ppermute(value, EVERY, pairs)


def seat():
    depth, row, col = (lax.axis_index(name) for name in EVERY)
    return (row // 2) * 2 + depth, row % 2, col // SIDE, col % SIDE


def held_at(step, mine):
    x, core, _, _ = seat()
    sign = 1 - 2 * core
    if mine:
        return group_index((x - sign * step + SIDE) % SIDE, core)
    return group_index((x + sign * step + SIDE) % SIDE, 1 - core)


def assemble(blocks, tokens, turn):
    arrays = []
    for array, _ in blocks.values():
        if not any(array is other for other in arrays):
            arrays.append(array)
    width = arrays[0].shape[-1]

    def kernel(*refs):
        out_ref = refs[len(arrays)]
        _, core, z, y = seat()
        for (r2, r1), (array, index) in blocks.items():
            ref = [r for r, other in zip(refs, arrays) if other is array][0]
            zz = (z + SIDE - jnp.where(core == 0, r2, r1)) % SIDE
            yy = (y + SIDE - jnp.where(core == 0, r1, r2)) % SIDE
            there = pl.ds(pl.multiple_of((zz * SIDE + yy) * width, width), width)
            lanes = pl.ds(pl.multiple_of((yy % 2) * width, width), width)
            out_ref[(zz * SIDE + yy) // 2, :, lanes] = ref[index]
            if turn:
                refs[-1][there, :] = ref[index].T

    return pl.pallas_call(
        kernel,
        out_shape=[
            jax.ShapeDtypeStruct(shape, jnp.bfloat16)
            for shape in ((8, tokens, 2 * width), (SIDE * SIDE * width, tokens))[: 1 + turn]
        ],
        in_specs=[VMEM] * len(arrays),
        out_specs=[VMEM] * (1 + turn),
        compiler_params=pltpu.CompilerParams(vmem_limit_bytes=18 * MIB),
        cost_estimate=LIGHT,
        name="assemble",
    )(*arrays)


def laid(parts):
    block, up, down, far0, far1 = parts
    blocks = {}
    for r1 in range(SIDE):
        blocks[0, r1] = (block, r1)
        blocks[1, r1] = (up, r1)
        blocks[2, r1] = (far0, r1) if r1 < 2 else (far1, r1 - 2)
        blocks[3, r1] = (down, r1)
    return blocks


def add(*values):
    return sum(v.astype(jnp.float32) for v in values).astype(jnp.bfloat16)


def forward(features, incoming, pieces, steps, wanted, carried, last):
    count = len(pieces)
    tokens = features.shape[1]
    _, rows, n = pieces[0].shape
    kinds = [m for m in range(3) if wanted[m]]
    given = [m for m in range(3) if carried[m] is not None]
    shared = wanted[0]

    def kernel(f_ref, g_ref, *refs):
        piece_refs, refs = refs[:count], refs[count:]
        carried_refs, refs = dict(zip(given, refs)), refs[len(given) :]
        outs, (f_held, g_held, w0, w1, w2, sems) = refs[:-6], refs[-6:]
        w_held = (w0, w1, w2)
        copies = [[], [], []]
        for m in kinds:
            for i, j in enumerate(wanted[m]):
                block = held_at(*steps[j])
                here = pl.ds(i * rows, rows)
                if m == 0:
                    copies[m].append((f_ref.at[block], f_held.at[:, here], sems.at[3, i]))
                if m == 2:
                    copies[m].append((g_ref.at[block], g_held.at[:, here], sems.at[4, i]))
                copies[m].append(
                    (piece_refs[j].at[m], w_held[m].at[here, :], sems.at[m, i])
                )
        copies = [[pltpu.make_async_copy(*c) for c in group] for group in copies]
        for group in copies:
            for c in group:
                c.start()
        results = []
        for m in kinds:
            for c in copies[m]:
                c.wait()
            result = matmul((g_held if m == 2 else f_held)[...], w_held[m][...])
            if m in given:
                result = result + carried_refs[m][...]
            if last:
                results.append(result)
            else:
                outs[len(results)][...] = result
                results.append(None)
        if last:
            gate_pre, up_pre, grad_hidden = results
            sigmoid_gate = jax.nn.sigmoid(gate_pre)
            activated = gate_pre * sigmoid_gate
            outs[0][...] = (activated * up_pre).astype(jnp.bfloat16)
            outs[1][:, :n] = (
                grad_hidden * up_pre * sigmoid_gate * (1.0 + gate_pre * (1.0 - sigmoid_gate))
            ).astype(jnp.bfloat16)
            outs[1][:, n:] = (grad_hidden * activated).astype(jnp.bfloat16)

    if last:
        out_shape = [
            jax.ShapeDtypeStruct((tokens, n), jnp.bfloat16),
            jax.ShapeDtypeStruct((tokens, 2 * n), jnp.bfloat16),
        ]
    else:
        out_shape = [jax.ShapeDtypeStruct((tokens, n), jnp.float32)] * len(kinds)
    depths = [max(len(w), 1) * rows for w in wanted]
    return pl.pallas_call(
        kernel,
        out_shape=out_shape,
        in_specs=[ANY] * 2 + [HBM] * count + [VMEM] * len(given),
        out_specs=[VMEM] * len(out_shape),
        scratch_shapes=[
            pltpu.VMEM((tokens, depths[0]), jnp.bfloat16),
            pltpu.VMEM((tokens, depths[2]), jnp.bfloat16),
        ]
        + [pltpu.VMEM((depth, n), jnp.bfloat16) for depth in depths]
        + [pltpu.SemaphoreType.DMA((5, count))],
        compiler_params=pltpu.CompilerParams(vmem_limit_bytes=22 * MIB),
        cost_estimate=LIGHT,
        name="forward_last" if last else "forward_part",
    )(features, incoming, *pieces, *(carried[m] for m in given))


def outer(turned, joined, steps):
    tokens, width = joined.shape
    count = len(steps)
    rows = turned.shape[0] // (SIDE * CORES)

    def kernel(t_ref, j_ref, first_ref, rest_ref, mine_ref, held, sems):
        now = pl.program_id(0)

        @pl.when(now == 0)
        def _():
            for i in range(count):
                for mine in (0, 1):
                    block = pl.ds(pl.multiple_of(held_at(steps[i], mine) * rows, rows), rows)
                    pltpu.make_async_copy(
                        t_ref.at[block, :], held.at[2 * i + mine], sems.at[2 * i + mine]
                    ).start()

        for mine in (0, 1):
            slot = 2 * now + mine
            pltpu.make_async_copy(
                t_ref.at[pl.ds(0, rows), :], held.at[slot], sems.at[slot]
            ).wait()
            result = matmul(held[slot], j_ref[...]).astype(jnp.bfloat16)
            if mine:
                mine_ref[0] = result
            else:

                @pl.when(now == 0)
                def _():
                    first_ref[...] = result

                @pl.when(now > 0)
                def _():
                    rest_ref[0] = result

    shape = lambda *dims: jax.ShapeDtypeStruct((*dims, rows, width), jnp.bfloat16)
    return pl.pallas_call(
        kernel,
        grid=(count,),
        out_shape=[shape(), shape(count - 1), shape(count)],
        in_specs=[ANY, pl.BlockSpec((tokens, width), lambda i: (0, 0))],
        out_specs=[
            pl.BlockSpec((rows, width), lambda i: (0, 0)),
            pl.BlockSpec((1, rows, width), lambda i: (jnp.maximum(i - 1, 0), 0, 0)),
            pl.BlockSpec((1, rows, width), lambda i: (i, 0, 0)),
        ],
        scratch_shapes=[
            pltpu.VMEM((2 * count, rows, tokens), jnp.bfloat16),
            pltpu.SemaphoreType.DMA((2 * count,)),
        ],
        compiler_params=pltpu.CompilerParams(vmem_limit_bytes=16 * MIB),
        cost_estimate=LIGHT,
        name="outer_product",
    )(turned, joined)


def partial_blocks(ahead, firsts, chunks, extra=None, extra_at=0):
    tokens = chunks[0][0].shape[0]
    widths = [hidden.shape[1] for hidden, _, _ in chunks]
    count = len(chunks[0][2])
    total = len(firsts)
    width = chunks[0][2][0].shape[1] // 2
    given = [] if extra is None else [extra]

    def kernel(*refs):
        act_refs, refs = refs[: 2 * len(chunks)], refs[2 * len(chunks) :]
        extra_refs, refs = refs[: len(given)], refs[len(given) :]
        piece_refs, refs = refs[: count * len(chunks)], refs[count * len(chunks) :]
        out_ref, *held, sems = refs
        now = pl.program_id(0)

        @pl.when(now == 0)
        def _():
            x, core, z, y = seat()
            sign = 1 - 2 * core
            for i, r in enumerate(firsts):
                zz = jnp.where(core == 0, z + ahead, z + r) % SIDE
                yy = jnp.where(core == 0, y + r, y + ahead) % SIDE
                block = (zz * SIDE + yy) // 2
                x_of = ((block % 4) // 2) * 2 + block // 4
                core_of = block % 2
                step = (sign * (x - x_of) + SIDE) % SIDE
                piece = jnp.where(core_of == core, step, SIDE + (SIDE - step) % SIDE)
                part = pl.ds(pl.multiple_of((yy % 2) * width, width), width)
                for p in range(count):

                    @pl.when(piece == p)
                    def _():
                        for c in range(len(chunks)):
                            pltpu.make_async_copy(
                                piece_refs[c * count + p].at[:, part, :],
                                held[c].at[i],
                                sems.at[c, i],
                            ).start()

        layer = grad = None
        for c, n in enumerate(widths):
            hid_ref, join_ref = act_refs[2 * c : 2 * c + 2]
            pltpu.make_async_copy(
                piece_refs[c * count].at[:, pl.ds(0, width), :], held[c].at[now], sems.at[c, now]
            ).wait()
            one = contract_last(hid_ref[...], held[c][now, 2])
            two = contract_last(join_ref[:, :n], held[c][now, 0])
            two = two + contract_last(join_ref[:, n:], held[c][now, 1])
            layer = one if layer is None else layer + one
            grad = two if grad is None else grad + two
        if given:
            counts = (now >= extra_at) & (now < extra_at + extra.shape[0])
            counts = jnp.where(counts, 1.0, 0.0)
            layer = layer + counts * extra_refs[0][0, 0].astype(jnp.float32)
            grad = grad + counts * extra_refs[0][0, 1].astype(jnp.float32)
        out_ref[0, 0] = layer.astype(jnp.bfloat16)
        out_ref[0, 1] = grad.astype(jnp.bfloat16)

    def extra_block(i):
        return jnp.clip(i - extra_at, 0, extra.shape[0] - 1), 0, 0, 0

    block = (1, 2, tokens, width)
    acts = [(act, pl.BlockSpec(act.shape, lambda i: (0, 0))) for c in chunks for act in c[:2]]
    return pl.pallas_call(
        kernel,
        grid=(total,),
        out_shape=jax.ShapeDtypeStruct((total, 2, tokens, width), jnp.bfloat16),
        in_specs=[s for _, s in acts]
        + [pl.BlockSpec(block, extra_block)] * len(given)
        + [HBM] * (count * len(chunks)),
        out_specs=pl.BlockSpec(block, lambda i: (i, 0, 0, 0)),
        scratch_shapes=[pltpu.VMEM((total, 3, width, n), jnp.bfloat16) for n in widths]
        + [pltpu.SemaphoreType.DMA((len(chunks), total))],
        compiler_params=pltpu.CompilerParams(vmem_limit_bytes=20 * MIB),
        cost_estimate=LIGHT,
        name="partial_blocks",
    )(*[act for act, _ in acts], *given, *[p for c in chunks for p in c[2]])


def body(tokens, gate_weight, up_weight, down_weight, cotangent):
    count = tokens.shape[0]
    weights = jnp.stack([gate_weight, up_weight, down_weight.T])
    own = [[weights[:, :, lo:hi]] for lo, hi in CUTS]
    sib = [[], []]
    early = [(s, m) for s in range(SIDE - 1) for m in (True, False)]
    late = [(SIDE - 1, m) for m in (True, False)]
    take = lambda c, steps: [(own if m else sib)[c][s] for s, m in steps]

    both = jnp.stack([tokens, cotangent])
    near = [both] + [plane(both, step, True) for step in (1, 2, -1)]
    own[0].append(ring(own[0][0]))

    over = (own[0][1], *near[1:])
    tok = [jnp.stack([v[0] for v in near])]
    own[0].append(ring(after(own[0][1], *over)))
    sib[0] += [sibling(after(own[0][s], *over)) for s in (0, 1)]
    tok += [plane(after(tok[0], *over), step, False) for step in (1, -1)]

    over = (own[0][2], *sib[0], *tok[1:])
    own[0].append(ring(after(own[0][2], *over)))
    tok.append(plane(after(tok[1][:2], *over), 1, False))
    tok.append(plane(after(tok[2][2:], *over), -1, False))
    sib[0].append(sibling(after(own[0][2], *tok[3:])))
    own[1].append(ring(after(own[1][0], own[0][3])))
    cot = [jnp.stack([v[1] for v in near])]
    cot += [plane(after(cot[0], *over), step, False) for step in (1, -1)]
    features, turned = assemble(laid(tok), count, True)
    steps = early + late
    most, rest, none = tuple(range(6)), (6, 7), (None,) * 3
    sums0 = forward(
        features, cot[0], take(0, early), early, (most, most, ()), none, False
    )
    cot.append(plane(after(cot[1][:2], features), 1, False))
    cot.append(plane(after(cot[2][2:], features), -1, False))

    over = (own[0][3], own[1][1], sib[0][2], *cot[3:], sums0[0])
    own[1].append(ring(after(own[1][1], *over)))
    sib[0].append(sibling(after(own[0][3], *over)))
    sib[1] += [sibling(after(own[1][s], *over, sib[0][3])) for s in (0, 1)]
    (incoming,) = assemble(laid(cot), count, False)
    hid0, join0 = forward(
        features,
        after(incoming, sib[0][3]),
        take(0, steps),
        steps,
        (rest, rest, most + rest),
        (*sums0, None),
        True,
    )
    first0, rest0, mine0 = outer(turned, join0, (1, 2, 3, 0))

    over = (own[1][2], mine0, *sib[1])
    own[1].append(ring(after(own[1][2], *over)))
    got0 = sibling(after(first0, *over))
    sib[1].append(sibling(after(own[1][2], *over)))
    sent0 = add(mine0[0], got0)
    chunk0 = (hid0, join0, own[0] + sib[0])
    sums1 = forward(
        after(features, sent0, sib[1][2]),
        incoming,
        take(1, early),
        early,
        (most,) * 3,
        none,
        False,
    )

    over = (own[1][3], sent0, *sib[1], sums1[0])
    sib[1].append(sibling(after(own[1][3], *over)))
    came0 = ring(sent0)
    got0 = sibling(after(rest0, *over, sib[1][3]))
    sums1 = (after(sums1[0], sib[1][3]), *sums1[1:])
    hid1, join1 = forward(features, incoming, take(1, late), late, ((0, 1),) * 3, sums1, True)
    chunk1 = (hid1, join1, own[1] + sib[1])

    def blocks(ahead, firsts, earlier, *extra):
        chunks = [(after(hid0, *earlier), *chunk0[1:]), chunk1]
        return partial_blocks(ahead, firsts, chunks, *extra)

    low = blocks(2, (0, 1), ())
    high = blocks(2, (2, 3), (low,))

    sent0 = add(mine0[1], got0[0], after(came0, high))

    over = (sent0, got0, high)
    far_up = plane(after(low, *over), 1, False)
    far_down = plane(after(high, *over), -1, False)
    came0 = ring(after(sent0, *over))
    first1, rest1, mine1 = outer(turned, after(join1, *over), (1, 2, 3, 0))
    got1 = sibling(first1)
    whole = tuple(range(SIDE))

    over = (came0, got1, far_up, far_down)
    sent0 = add(mine0[2], got0[1], after(came0, *over))
    sent1 = add(mine1[0], after(got1, *over))
    came0, came1 = ring(sent0), ring(sent1)
    got1 = sibling(after(rest1, *over))
    behind = blocks(1, whole, (sent0, sent1), far_up, 0)
    up = plane(behind, 1, False)
    front = blocks(3, whole, (behind, got1), far_down, 2)
    down = plane(front, -1, False)
    here = blocks(0, whole, (front,))

    over = (came0, came1, here)
    sent1 = add(mine1[1], got1[0], after(came1, *over))
    came1 = ring(sent1)
    total = add(here, after(up, sent1), down)
    came_near = [plane(total[r1], step, True) for r1, step in ((1, 1), (2, 2), (3, -1))]
    sent1 = add(mine1[2], got1[1], came1)
    came1 = ring(sent1)

    scale = 1.0 / (count * SIDE * CORES) ** 0.5
    grads = [
        sum(v.astype(jnp.float32) for v in terms) * scale
        for terms in ((mine0[3], got0[2], came0), (mine1[3], got1[2], came1))
    ]
    widths = [hi - lo for lo, hi in CUTS]
    grad_gate = jnp.concatenate([g[:, :n] for g, n in zip(grads, widths)], axis=1)
    grad_up = jnp.concatenate([g[:, n:] for g, n in zip(grads, widths)], axis=1)
    total = after(total[0], grad_gate, grad_up)
    layer_out, grad_tokens = [add(total[i], *(v[i] for v in came_near)) for i in range(2)]
    return (layer_out, grad_tokens, grad_gate, grad_up)


def solution(mesh):
    in_specs = (
        P(("depth", "row"), "col"),
        P(("depth", "row"), "col"),
        P(("depth", "row"), "col"),
        P("col", ("depth", "row")),
        P(("depth", "row"), "col"),
    )
    out_specs = (
        P(("depth", "row"), "col"),
        P(("depth", "row"), "col"),
        P(("depth", "row"), "col"),
        P(("depth", "row"), "col"),
    )
    return jax.shard_map(body, mesh=mesh, in_specs=in_specs, out_specs=out_specs, check_vma=False)
```
